128 devices in a mesh: row: 8 (over y, x_lo), col: 16 (over x_hi, z, core).
Axes of the slice: x: 4 (x_hi: 2, x_lo: 2; x = x_hi * 2 + x_lo), y: 4, z: 4, core: 2. Of those that a mesh axis runs over, the one named last changes fastest.
Arguments:
- apanel: bfloat16 [32768, 16384], P('row', 'col'), may hold values from -6 to 6
- rowmask: int32 [256, 16], P('row', 'col'), may hold values from 0 to 1, as said below
- qpanel: bfloat16 [2, 8192, 16384], P(None, 'row', 'col'), may hold values from -0.109375 to 0.109375
Outputs:
- product: bfloat16 [32768, 16384], P('row', 'col')
The draws below stay inside these ranges and needn't reach their ends.
Inputs may be any that keep to these rules, and one draw needn't show every extreme that they name: `rowmask`: write k = (i + j) mod 16 for column j of tile row i (rows i*32 to i*32 + 31). Tiles with k less than half of 16 have 1 to 24 entries equal to 1 in their column; the others 1 to 8. In every tile row the tile with k = 0 has exactly 24 and the tile with k equal to half of 16 exactly 8.
All inputs are finite; a program needn't handle non-finite values.
Results may differ from the reference program's by a relative error of at most 0.004.
Values may be sent and summed in bfloat16 or wider, within the bound.
A program may use at most 256 MiB of HBM per device.

```python
import jax
import jax.numpy as jnp
from jax import lax

BS = 128
LR = 32
LK = 8
LC = 8
SHIFTS = 3
GRID_ROWS = 8
PANELS = 16
ROWS = 32768
INNER = 16384
COLS = 16384
MAXNZ = 24
LIGHTNZ = 8


def draw_rowmask(key, part):
    key = jax.random.fold_in(key, 11)
    count_key, order_key = jax.random.split(key)
    tile_rows = jnp.arange(GRID_ROWS, dtype=jnp.int32)[:, None]
    tile_cols = jnp.arange(PANELS, dtype=jnp.int32)[None, :]
    panel = (tile_rows + tile_cols) % PANELS
    dense_count = jax.random.randint(count_key, (GRID_ROWS, PANELS), 1, MAXNZ + 1)
    sparse_count = jax.random.randint(jax.random.fold_in(count_key, 1), (GRID_ROWS, PANELS), 1, LIGHTNZ + 1)
    counts = jnp.where(panel < PANELS // 2, dense_count, sparse_count)
    counts = jnp.where(panel == 0, MAXNZ, counts)
    counts = jnp.where(panel == PANELS // 2, LIGHTNZ, counts)
    scores = jax.random.randint(order_key, (GRID_ROWS, PANELS, LR), 0, 1 << 20)
    scores = scores * LR + jnp.arange(LR, dtype=jnp.int32)
    ranks = jnp.argsort(jnp.argsort(scores, axis=-1), axis=-1)
    row_flags = (ranks < counts[:, :, None]).astype(jnp.int32)
    return jnp.transpose(row_flags, (0, 2, 1)).reshape(GRID_ROWS * LR, PANELS)


def level_of(key, extent, cuts, low, high):
    def one(dim, shards_of):
        steps = jax.random.uniform(jax.random.fold_in(jax.random.fold_in(key, 6), dim), (shards_of,), jnp.float32, low / len(cuts), high / len(cuts))
        return jnp.repeat(jnp.exp(steps), extent[dim] // shards_of).reshape((-1,) + (1,) * (len(extent) - dim - 1))

    factor_of = one(*cuts[0])
    for cut in cuts[1:]:
        factor_of = factor_of * one(*cut)
    return factor_of


def gaussian(key, extent, scale, reach, shards=(), held_as=jnp.bfloat16):
    factor_of = level_of(key, extent, shards, -0.22, 0.18) if shards else 1.0
    values = jax.random.normal(key, extent, jnp.float32) * scale * factor_of
    return jnp.minimum(jnp.maximum(values, -reach), reach).astype(held_as)


def setup_inputs(seed: int = 0) -> dict:
    splits = jax.random.split(jax.random.key(seed), 4)
    return {
        "apanel": gaussian(splits[0], (ROWS, INNER), 1.0, 6.0, ((0, 8), (1, 16))),
        "rowmask": draw_rowmask(jax.random.fold_in(splits[3], 71), 0),
        "qpanel": gaussian(splits[2], (2, GRID_ROWS * LK * BS, COLS), (SHIFTS * LK * BS) ** -0.5, 0.109375, ((1, 8), (2, 16))),
    }


def reference(apanel, rowmask, qpanel):
    occupied = (rowmask > 0).reshape(GRID_ROWS, LR, 1, PANELS, 1)
    band = apanel.reshape(GRID_ROWS, LR, BS, PANELS, LK * BS)
    masked = jnp.where(occupied, band, jnp.zeros((), band.dtype))
    stacked = qpanel.reshape(2 * GRID_ROWS, LK * BS, PANELS, LC * BS)

    def tile_row(group):
        own_band = lax.dynamic_index_in_dim(masked, group, 0, keepdims=False).astype(jnp.float32)
        totals = jnp.zeros((LR, BS, PANELS, LC * BS), jnp.float32)
        for offset in range(SHIFTS):
            rolled = jnp.roll(own_band, -offset, axis=2)
            factor = lax.dynamic_index_in_dim(stacked, (group + offset) % PANELS, 0, keepdims=False).astype(jnp.float32)
            totals = totals + jnp.einsum("rbjk,kjc->rbjc", rolled, factor)
        return totals.astype(jnp.bfloat16)

    result = lax.map(tile_row, jnp.arange(GRID_ROWS, dtype=jnp.int32))
    return result.reshape(GRID_ROWS * LR * BS, PANELS * LC * BS)
```

```python
import jax
import jax.numpy as jnp
from jax import lax
from jax.experimental import pallas as pl
from jax.experimental.pallas import tpu as pltpu
from jax.sharding import PartitionSpec as P

BS = 128
LR = 32
WIDTH = 1024
MAXNZ = 24
LIGHTNZ = 8
PANELS = 16
GRID_ROWS = 8
GROUP = 4
GROUPS = MAXNZ // GROUP
QPARTS = WIDTH // BS
MESH = pl.DeviceIdType.MESH

OUT = [
    [
        262, 262, 518, 518, 12550, 12550, 8, 8, 8962, 8962, 8708, 8708, 0, 0, 0, 0,
        4614, 4614, 4710, 4710, 4102, 4102, 8866, 8866, 12834, 12834, 0, 0, 0, 0, 12360, 0,
        1286, 1286, 1544, 1544, 1028, 1028, 0, 0, 9986, 9986, 0, 0, 0, 0, 9223, 9223,
        5382, 5382, 5734, 5734, 0, 9508, 0, 0, 14082, 14082, 0, 0, 13378, 13378, 13414, 13414,
        2566, 2566, 2661, 2661, 2049, 2049, 0, 0, 10754, 10754, 0, 0, 6405, 6405, 10326, 10326,
        6726, 6726, 6818, 6818, 0, 0, 0, 0, 14882, 14882, 10792, 14914, 2311, 2311, 14393, 14393,
        3590, 3590, 0, 0, 3074, 3074, 0, 0, 12034, 12034, 11784, 11784, 7430, 7430, 11270, 11270,
        7752, 12072, 0, 0, 0, 0, 0, 0, 3364, 15880, 3108, 3108, 3430, 3430, 3686, 3686,
    ],
    [
        774, 774, 12292, 12292, 8452, 8452, 12802, 12802, 0, 0, 0, 0, 0, 0, 0, 0,
        4870, 4870, 8196, 8196, 8258, 8258, 0, 0, 0, 0, 0, 0, 0, 0, 0, 0,
        1798, 1798, 13922, 13922, 13316, 13316, 0, 0, 0, 0, 0, 0, 0, 0, 5123, 5123,
        5638, 5638, 9732, 9732, 0, 0, 0, 0, 0, 0, 0, 0, 0, 0, 1668, 1668,
        2822, 2822, 14339, 14339, 0, 0, 0, 0, 0, 0, 0, 0, 10245, 10245, 6660, 6660,
        6918, 6918, 0, 0, 0, 0, 0, 0, 0, 0, 0, 0, 2066, 2066, 2737, 2737,
        3846, 3846, 0, 0, 0, 0, 0, 0, 0, 0, 7170, 7170, 3330, 3330, 7684, 7684,
        7944, 0, 0, 0, 0, 0, 0, 0, 15876, 3364, 15940, 16004, 15364, 15364, 15428, 15428,
    ],
    [
        13062, 13062, 0, 0, 0, 0, 0, 0, 0, 0, 0, 0, 0, 0, 0, 0,
        8774, 8774, 0, 0, 8514, 8514, 0, 0, 0, 0, 0, 0, 0, 0, 0, 0,
        13830, 13830, 0, 0, 9474, 9474, 0, 0, 0, 0, 0, 0, 0, 0, 0, 0,
        5894, 5894, 0, 0, 0, 0, 0, 0, 0, 0, 0, 0, 0, 0, 0, 0,
        15110, 15110, 14850, 14850, 0, 0, 0, 0, 0, 0, 0, 0, 0, 0, 0, 0,
        11014, 11014, 0, 0, 0, 0, 0, 0, 0, 0, 0, 0, 6481, 6481, 0, 0,
        16134, 16134, 0, 0, 0, 0, 0, 0, 0, 0, 0, 0, 7202, 7202, 0, 0,
        0, 0, 0, 0, 0, 0, 0, 0, 0, 0, 3938, 3938, 0, 0, 0, 0,
    ],
]
IN = [
    [
        1032, 1032, 17926, 17926, 6, 6, 18022, 18022, 8292, 8292, 612, 612, 16388, 16388, 1538, 1538,
        8710, 8710, 0, 0, 26118, 26118, 26214, 26214, 100, 100, 518, 518, 1154, 1154, 18118, 18118,
        2564, 2564, 19974, 19974, 2056, 2056, 20070, 20070, 19463, 19463, 2690, 2690, 10340, 10340, 3586, 3586,
        19571, 19571, 28166, 28166, 28262, 28262, 28358, 28358, 2628, 2628, 0, 0, 20166, 20166, 11778, 11778,
        4609, 4609, 29191, 29191, 22022, 22022, 22118, 22118, 21077, 21077, 0, 0, 5634, 5634, 30406, 30406,
        0, 0, 20997, 20997, 21604, 21604, 30310, 30310, 4179, 4179, 0, 0, 4226, 4226, 22214, 22214,
        6658, 6658, 23138, 23138, 24070, 24070, 24166, 24166, 23558, 23558, 0, 0, 22536, 22536, 7682, 7682,
        22658, 22658, 23046, 23046, 23652, 23652, 32392, 0, 31332, 31332, 0, 0, 15940, 15880, 24262, 24262,
    ],
    [
        0, 0, 0, 0, 0, 0, 0, 0, 8802, 8802, 8834, 8834, 26310, 26310, 0, 0,
        0, 0, 0, 0, 8198, 8198, 0, 0, 25608, 0, 0, 0, 9730, 9730, 0, 0,
        0, 0, 0, 0, 27748, 27748, 0, 0, 0, 0, 0, 10756, 0, 0, 0, 0,
        0, 0, 0, 0, 10246, 10246, 0, 0, 27138, 27138, 0, 0, 2178, 2178, 0, 0,
        29298, 29298, 0, 0, 4101, 4101, 0, 0, 21510, 21510, 0, 0, 28680, 0, 0, 0,
        0, 0, 29329, 29329, 30214, 30214, 0, 0, 29705, 29705, 0, 0, 13826, 13826, 0, 0,
        30724, 30724, 15876, 16004, 31750, 31750, 30850, 30850, 0, 0, 0, 0, 0, 0, 0, 32264,
        23170, 23170, 0, 0, 32264, 0, 0, 0, 31844, 31844, 0, 0, 30788, 30788, 0, 0,
    ],
    [
        0, 0, 0, 0, 0, 0, 0, 0, 0, 0, 0, 0, 9218, 9218, 0, 0,
        0, 0, 0, 0, 0, 0, 0, 0, 0, 0, 0, 0, 0, 0, 0, 0,
        0, 0, 0, 0, 0, 0, 0, 0, 0, 0, 0, 0, 0, 0, 0, 0,
        0, 0, 0, 0, 0, 0, 0, 0, 27654, 27654, 0, 0, 0, 0, 0, 0,
        0, 0, 0, 0, 29841, 29841, 0, 0, 0, 0, 0, 0, 0, 0, 0, 0,
        0, 0, 0, 0, 12290, 12290, 0, 0, 0, 0, 0, 0, 0, 28674, 0, 0,
        0, 0, 31238, 31238, 0, 0, 0, 0, 0, 0, 0, 0, 0, 0, 0, 0,
        0, 0, 0, 0, 0, 0, 0, 0, 0, 0, 0, 0, 0, 0, 0, 0,
    ],
]
SLOTS = 12


def pick(values, at):
    bit = 1
    while len(values) > 1:
        odd = (at // bit) % 2 == 1
        values = [
            a if isinstance(a, int) and isinstance(b, int) and a == b else jnp.where(odd, b, a)
            for a, b in zip(values[::2], values[1::2])
        ]
        bit *= 2
    return jnp.int32(values[0]) if isinstance(values[0], int) else values[0]


def on_chip(chip, core):
    x, y, z = chip // 16, (chip // 4) % 4, chip % 4
    return {"row": y * 2 + x % 2, "col": (x // 2) * 8 + z * 2 + core}


def chunks_of(row, col):
    return jnp.where((row + col) % PANELS < PANELS // 2, MAXNZ, LIGHTNZ)


def kernel(
    band, flags, qtiles, product, raw, tiles, relay, factors, parts, flags1, flags2, ranks, following, slots,
    load_sem, own_send, pair_send, relay_send, q_send, q_fwd, flag_send, got1, got2, relay_got, q_got1, q_got2, flag_got, out_sem,
):
    row, col = lax.axis_index("row"), lax.axis_index("col")
    core = col % 2
    odd_row = row % 2
    back1, back2 = (col + PANELS - 1) % PANELS, (col + PANELS - 2) % PANELS
    ahead1, ahead2 = (col + 1) % PANELS, (col + 2) % PANELS
    pair = {"row": row, "col": col + 1 - 2 * core}
    behind = {"row": row, "col": back2}
    row_behind, row_ahead = (row + GRID_ROWS - 2) % GRID_ROWS, (row + 2) % GRID_ROWS
    row_pair = {"row": row + 1 - 2 * odd_row, "col": col}
    n0, n1, n2 = chunks_of(row, col), chunks_of(row, ahead1), chunks_of(row, ahead2)

    load_raw = pltpu.make_async_copy(band, raw, load_sem.at[0])
    load_raw.start()
    load_q = pltpu.make_async_copy(qtiles.at[0], factors.at[0], load_sem.at[1])
    load_q.start()

    me = row * PANELS + col
    outs = []
    first = 0
    for table in OUT:
        code = pick(table, me)
        outs.append((code // 256, (code // 16) % 16, first, code % 16))
        first = first + code % 16
    straight = first
    ins = []
    slot = 0
    for table in IN:
        code = pick(table, me)
        ins.append((code // 512, (code // 16) % 32, slot, code % 16))
        slot = slot + code % 16

    barrier = pltpu.get_barrier_semaphore()

    def greet(device):
        pl.semaphore_signal(barrier, inc=1, device_id=device, device_id_type=MESH)

    for device in ({"row": row, "col": ahead1}, {"row": row, "col": ahead2}, pair, {"row": row_ahead, "col": col}, row_pair):
        greet(device)
    expected = 5
    for chip, _, _, count in outs:
        expected = expected + jnp.where(count > 0, 1, 0)
    for chip, _, _, count in ins:
        expected = expected + jnp.where(count > 0, 1, 0)
        target = on_chip(chip, core)

        @pl.when(count > 0)
        def _():
            greet({"row": target["row"], "col": (target["col"] + 2) % PANELS})

    for table in OUT:
        code = pick(table, row * PANELS + ahead2)

        @pl.when(code > 0)
        def _():
            greet(on_chip(code // 256, core))

    following[LR] = LR - 1

    @pl.loop(0, LR)
    def _(t):
        r = LR - 1 - t
        following[r] = jnp.where(flags[r] > 0, r, following[r + 1])

    @pl.loop(0, MAXNZ)
    def _(t):
        before = jnp.where(t == 0, -1, slots[jnp.maximum(t - 1, 0)])
        slots[t] = following[before + 1]

    def remote(src, dst, send, recv, device):
        return pltpu.make_async_remote_copy(
            src_ref=src, dst_ref=dst, send_sem=send, recv_sem=recv, device_id=device, device_id_type=MESH
        )

    def landed(dst, sem):
        pltpu.make_async_copy(dst, dst, sem).wait()

    pl.semaphore_wait(barrier, expected)

    wrapped = jnp.where(row < 2, 1, 0)

    def q_rows(u):
        return pl.ds(u * BS if isinstance(u, int) else pl.multiple_of(u * BS, BS), BS)

    def q_copy(u):
        return remote(
            qtiles.at[wrapped, q_rows(u)], factors.at[2, q_rows(u)], q_send.at[u], q_got2.at[u], {"row": row_behind, "col": col}
        )

    def q_pair_own(u):
        return remote(qtiles.at[0, q_rows(u)], factors.at[1, q_rows(u)], q_fwd.at[u], q_got1.at[u], row_pair)

    def q_pair_forward(u):
        return remote(factors.at[2, q_rows(u)], factors.at[1, q_rows(u)], q_fwd.at[u], q_got1.at[u], row_pair)

    flag_copies = [
        remote(flags, flags1, flag_send.at[0], flag_got.at[0], {"row": row, "col": back1}),
        remote(flags, flags2, flag_send.at[1], flag_got.at[1], behind),
    ]
    for copy in flag_copies:
        copy.start()

    @pl.loop(0, QPARTS)
    def _(u):
        q_copy(u).start()

        @pl.when(odd_row == 1)
        def _():
            q_pair_own(u).start()

    load_raw.wait()

    @pl.loop(0, MAXNZ)
    def _(t):
        @pl.when(t < n0)
        def _():
            tiles[0, t] = raw[slots[t]]

    def own_copy(t):
        return remote(tiles.at[0, t], tiles.at[2, t], own_send.at[t], got2.at[t], behind)

    def own_to_relay(t, chip, at):
        return remote(tiles.at[0, t], relay.at[at], own_send.at[t], relay_got.at[at], on_chip(chip, core))

    def own_to_pair(t):
        return remote(tiles.at[0, t], tiles.at[1, t], pair_send.at[t], got1.at[t], pair)

    def forward_to_pair(t):
        return remote(tiles.at[2, t], tiles.at[1, t], pair_send.at[t], got1.at[t], pair)

    def pass_on(at, chip, t):
        return remote(relay.at[at], tiles.at[2, t], relay_send.at[at], got2.at[t], on_chip(chip, core))

    @pl.loop(0, MAXNZ)
    def _(u):
        for chip, at, t, count in outs:
            @pl.when(u < count)
            def _():
                own_to_relay(t + u, chip, at + u).start()

        @pl.when(u < n0 - straight)
        def _():
            own_copy(straight + u).start()

    @pl.when(core == 1)
    def _():
        @pl.loop(0, n0)
        def _(t):
            own_to_pair(t).start()

    load_q.wait()

    def multiply(s, v):
        lhs = tiles[s, pl.ds(v * GROUP, GROUP)].reshape(GROUP * BS, WIDTH)
        out = jnp.dot(lhs, factors[s], preferred_element_type=jnp.float32)
        parts[s, pl.ds(v * GROUP, GROUP)] = out.astype(jnp.bfloat16).reshape(GROUP, BS, WIDTH)

    @pl.loop(0, GROUPS)
    def _(v):
        @pl.loop(v * GROUP, (v + 1) * GROUP)
        def _(u):
            @pl.when((odd_row == 0) & (u < QPARTS))
            def _():
                landed(factors.at[2, q_rows(u)], q_got2.at[u])
                q_pair_forward(u).start()

            for chip, t, at, count in ins:
                @pl.when(u < count)
                def _():
                    landed(relay.at[at + u], relay_got.at[at + u])
                    pass_on(at + u, chip, t + u).start()

        @pl.when(v * GROUP < n0)
        def _():
            multiply(0, v)

    @pl.loop(0, QPARTS)
    def _(u):
        landed(factors.at[1, q_rows(u)], q_got1.at[u])

        @pl.when(odd_row == 1)
        def _():
            landed(factors.at[2, q_rows(u)], q_got2.at[u])

    def take1(v):
        @pl.loop(v * GROUP, (v + 1) * GROUP)
        def _(u):
            landed(tiles.at[1, u], got1.at[u])

        multiply(1, v)

    @pl.loop(0, GROUPS)
    def _(v):
        @pl.when((core == 0) & (v * GROUP < n1))
        def _():
            take1(v)

        @pl.when(v * GROUP < n2)
        def _():
            @pl.loop(v * GROUP, (v + 1) * GROUP)
            def _(u):
                landed(tiles.at[2, u], got2.at[u])

                @pl.when(core == 0)
                def _():
                    forward_to_pair(u).start()

            multiply(2, v)

        @pl.when((core == 1) & (v * GROUP < n1))
        def _():
            take1(v)

    for copy in flag_copies:
        copy.wait()
    for s, (held, n) in enumerate(((flags, n0), (flags1, n1), (flags2, n2))):
        def place(r, count):
            ranks[s, r] = jnp.minimum(count, n - 1)
            return count + held[r]

        lax.fori_loop(0, LR, place, jnp.int32(0))

    @pl.loop(0, LR)
    def _(r):
        there = [held[r] > 0 for held in (flags, flags1, flags2)]
        at = [ranks[s, r] for s in range(3)]

        @pl.loop(0, BS, step=16)
        def _(h):
            lines = pl.ds(pl.multiple_of(h, 16), 16)
            total = jnp.zeros((16, WIDTH), jnp.float32)
            for s in range(3):
                total += jnp.where(there[s], parts[s, at[s], lines].astype(jnp.float32), 0.0)
            raw[r, lines] = total.astype(jnp.bfloat16)

        pltpu.make_async_copy(raw.at[r], product.at[r], out_sem.at[0]).start()

    @pl.loop(0, QPARTS)
    def _(u):
        q_copy(u).wait_send()

        @pl.when(odd_row == 1)
        def _():
            q_pair_own(u).wait_send()

        @pl.when(odd_row == 0)
        def _():
            q_pair_forward(u).wait_send()

    @pl.loop(0, n0)
    def _(t):
        own_copy(t).wait_send()

    @pl.loop(0, jnp.where(core == 0, n2, n0))
    def _(t):
        own_to_pair(t).wait_send()

    @pl.loop(0, slot)
    def _(at):
        pass_on(at, 0, 0).wait_send()

    pltpu.make_async_copy(raw, product, out_sem.at[0]).wait()


def per_device(apanel, rowmask, qpanel):
    dma = pltpu.SemaphoreType.DMA
    whole = pl.BlockSpec(memory_space=pl.ANY)
    product = pl.pallas_call(
        kernel,
        out_shape=jax.ShapeDtypeStruct((LR, BS, WIDTH), jnp.bfloat16),
        in_specs=[whole, pl.BlockSpec(memory_space=pltpu.SMEM), whole],
        out_specs=whole,
        scratch_shapes=[
            pltpu.VMEM((LR, BS, WIDTH), jnp.bfloat16),
            pltpu.VMEM((3, MAXNZ, BS, WIDTH), jnp.bfloat16),
            pltpu.VMEM((SLOTS, BS, WIDTH), jnp.bfloat16),
            pltpu.VMEM((3, WIDTH, WIDTH), jnp.bfloat16),
            pltpu.VMEM((3, MAXNZ, BS, WIDTH), jnp.bfloat16),
            pltpu.SMEM((LR,), jnp.int32),
            pltpu.SMEM((LR,), jnp.int32),
            pltpu.SMEM((3, LR), jnp.int32),
            pltpu.SMEM((LR + 1,), jnp.int32),
            pltpu.SMEM((LR,), jnp.int32),
            dma((2,)),
            dma((MAXNZ,)),
            dma((MAXNZ,)),
            dma((SLOTS,)),
            dma((QPARTS,)),
            dma((QPARTS,)),
            dma((2,)),
            dma((MAXNZ,)),
            dma((MAXNZ,)),
            dma((SLOTS,)),
            dma((QPARTS,)),
            dma((QPARTS,)),
            dma((2,)),
            dma((1,)),
        ],
        compiler_params=pltpu.CompilerParams(collective_id=0, has_side_effects=True, vmem_limit_bytes=60 << 20),
    )(apanel.reshape(LR, BS, WIDTH), rowmask.reshape(LR), qpanel)
    return product.reshape(LR * BS, WIDTH)


def solution(mesh):
    in_specs = (P("row", "col"), P("row", "col"), P(None, "row", "col"))
    return jax.shard_map(per_device, mesh=mesh, in_specs=in_specs, out_specs=P("row", "col"), check_vma=False)
```

```python
import jax
import jax.numpy as jnp
from jax import lax
from jax.experimental import pallas as pl
from jax.experimental.pallas import tpu as pltpu
from jax.sharding import PartitionSpec as P

BS = 128
LR = 32
WIDTH = 1024
MAXNZ = 24
LIGHTNZ = 8
PANELS = 16
GRID_ROWS = 8
GROUP = 4
GROUPS = MAXNZ // GROUP
QPARTS = WIDTH // BS
MESH = pl.DeviceIdType.MESH

OUT = [
    [
        518, 518, 12806, 12806, 5, 5, 1540, 1540, 4865, 4865, 0, 0, 0, 0, 0, 0,
        4614, 4614, 7174, 7174, 4102, 4102, 5634, 0, 13137, 13137, 0, 0, 0, 0, 12322, 0,
        1798, 1798, 13318, 13318, 1030, 1030, 0, 0, 9729, 9729, 0, 0, 0, 0, 9222, 9222,
        5894, 5894, 9318, 9318, 5122, 0, 0, 0, 13825, 13825, 0, 0, 9474, 0, 13414, 13414,
        2822, 2822, 2596, 2596, 0, 0, 0, 0, 11009, 11009, 0, 0, 9509, 9477, 6741, 6741,
        6918, 6918, 0, 6818, 0, 0, 0, 0, 15105, 15105, 0, 13842, 2405, 2405, 2662, 2662,
        3638, 3638, 0, 0, 0, 0, 0, 0, 8017, 8017, 8198, 8198, 7430, 7430, 11270, 11270,
        12044, 0, 0, 0, 0, 0, 0, 0, 0, 16140, 12374, 12342, 12550, 12550, 15366, 15366,
    ],
    [
        774, 774, 3075, 3075, 3332, 3332, 3587, 3587, 0, 0, 0, 0, 0, 0, 0, 0,
        8966, 8966, 8707, 8707, 8451, 8451, 0, 0, 0, 0, 0, 0, 0, 0, 0, 0,
        14086, 14086, 2562, 2562, 6402, 6402, 0, 0, 0, 0, 0, 0, 0, 0, 8755, 8755,
        9990, 9990, 6659, 6659, 0, 0, 0, 0, 0, 0, 0, 0, 0, 0, 1698, 1698,
        14854, 14854, 3123, 3123, 0, 0, 0, 0, 0, 0, 0, 0, 6434, 6434, 10276, 10276,
        10758, 10758, 0, 0, 0, 0, 0, 0, 0, 0, 0, 0, 14339, 14339, 14387, 14387,
        3846, 3846, 0, 0, 0, 0, 0, 0, 0, 0, 10338, 10338, 8499, 8499, 8803, 8803,
        7686, 0, 0, 0, 0, 0, 0, 0, 0, 15878, 15875, 15971, 3394, 3394, 3731, 3731,
    ],
    [
        13061, 13061, 0, 0, 0, 0, 12290, 12290, 0, 0, 0, 0, 0, 0, 0, 0,
        4885, 4885, 0, 0, 0, 0, 0, 0, 0, 0, 0, 0, 0, 0, 0, 0,
        1605, 1605, 1681, 1681, 2305, 2305, 0, 0, 0, 0, 0, 0, 0, 0, 0, 0,
        5669, 5637, 0, 0, 0, 0, 0, 0, 0, 0, 0, 0, 0, 0, 12353, 12321,
        2325, 2325, 6706, 6706, 0, 0, 0, 0, 0, 0, 0, 0, 10242, 10242, 0, 0,
        7941, 7941, 0, 0, 0, 0, 0, 0, 0, 0, 0, 0, 6465, 6465, 0, 0,
        15125, 15125, 0, 0, 0, 0, 0, 0, 0, 0, 11777, 11777, 0, 0, 0, 0,
        0, 0, 0, 0, 0, 0, 0, 0, 0, 0, 0, 0, 3169, 3169, 0, 0,
    ],
]
IN = [
    [
        821, 821, 0, 0, 18214, 18214, 18118, 18118, 22822, 22822, 8947, 8947, 8435, 8435, 26310, 26310,
        8998, 8998, 0, 0, 26406, 26406, 1649, 1649, 1266, 1266, 31526, 31526, 294, 294, 18037, 18037,
        2854, 2854, 0, 0, 1348, 1348, 20262, 20262, 19750, 19750, 27234, 21301, 3697, 3697, 28358, 28358,
        11106, 0, 0, 0, 9570, 28277, 28454, 28454, 2342, 2342, 0, 0, 11889, 11889, 20166, 20166,
        0, 0, 2801, 2801, 2306, 2306, 22310, 22310, 21234, 21234, 0, 0, 30406, 30406, 5745, 5745,
        0, 0, 2818, 2818, 10483, 10483, 30502, 30502, 29443, 29443, 0, 0, 22214, 22214, 13937, 13937,
        243, 243, 756, 756, 1299, 1299, 24262, 24262, 23846, 23846, 0, 0, 22769, 22769, 32460, 0,
        8486, 8486, 23334, 23334, 32358, 0, 30325, 30325, 32038, 32038, 0, 0, 30963, 15974, 0, 16076,
    ],
    [
        0, 0, 0, 0, 0, 0, 0, 0, 0, 0, 23283, 23283, 19699, 19699, 0, 0,
        0, 0, 0, 0, 0, 0, 26229, 26229, 25698, 27889, 0, 0, 0, 0, 9841, 9841,
        0, 0, 0, 0, 20085, 20085, 0, 0, 10534, 10534, 21301, 0, 0, 0, 0, 0,
        0, 0, 0, 0, 28277, 0, 0, 0, 27942, 27942, 0, 0, 0, 29026, 0, 0,
        0, 0, 22133, 22133, 4420, 4420, 0, 0, 21748, 21748, 0, 0, 0, 0, 0, 0,
        0, 0, 21266, 21266, 4338, 4338, 0, 0, 29939, 29939, 0, 0, 0, 0, 24181, 24181,
        4371, 4371, 31490, 31490, 24358, 24358, 0, 0, 0, 0, 0, 0, 0, 0, 0, 0,
        0, 0, 0, 0, 0, 0, 7793, 7793, 0, 0, 0, 0, 0, 30963, 0, 0,
    ],
    [
        0, 0, 0, 0, 0, 0, 0, 0, 0, 0, 0, 0, 23795, 23795, 0, 0,
        0, 0, 0, 0, 0, 0, 0, 0, 27889, 31014, 0, 0, 0, 0, 0, 0,
        0, 0, 0, 0, 2289, 2289, 0, 0, 0, 0, 0, 0, 0, 0, 0, 0,
        0, 0, 0, 0, 0, 0, 0, 0, 0, 0, 0, 0, 0, 0, 0, 0,
        0, 0, 29493, 29493, 29990, 29990, 0, 0, 22786, 22786, 0, 0, 0, 0, 0, 0,
        0, 0, 29425, 29425, 21813, 21813, 0, 0, 0, 0, 0, 0, 0, 0, 0, 0,
        31473, 31473, 0, 0, 31987, 31987, 0, 0, 0, 0, 0, 0, 0, 0, 0, 0,
        0, 0, 0, 0, 0, 0, 0, 0, 0, 0, 0, 0, 0, 0, 0, 0,
    ],
    [
        0, 0, 0, 0, 0, 0, 0, 0, 0, 0, 0, 0, 0, 0, 0, 0,
        0, 0, 0, 0, 0, 0, 0, 0, 31014, 0, 0, 0, 0, 0, 0, 0,
        0, 0, 0, 0, 27906, 27906, 0, 0, 0, 0, 0, 0, 0, 0, 0, 0,
        0, 0, 0, 0, 0, 0, 0, 0, 0, 0, 0, 0, 0, 0, 0, 0,
        0, 0, 0, 0, 0, 0, 0, 0, 0, 0, 0, 0, 0, 0, 0, 0,
        0, 0, 0, 0, 0, 12386, 0, 0, 0, 0, 0, 0, 0, 0, 0, 0,
        0, 0, 0, 0, 0, 0, 0, 0, 0, 0, 0, 0, 0, 0, 0, 0,
        0, 0, 0, 0, 0, 0, 0, 0, 0, 0, 0, 0, 0, 0, 0, 0,
    ],
]
SLOTS = 12

TICKS = 12
Q_TICKS = 8
RELAY_TICKS = 8
STRAIGHT_TICKS = 10
LAG = 1
STRAIGHT_LAG = 2
TICK2 = Q_TICKS + LAG
TICK1 = TICK2 + LAG + 1


def pick(values, at):
    bit = 1
    while len(values) > 1:
        odd = (at // bit) % 2 == 1
        values = [
            a if isinstance(a, int) and isinstance(b, int) and a == b else jnp.where(odd, b, a)
            for a, b in zip(values[::2], values[1::2])
        ]
        bit *= 2
    return jnp.int32(values[0]) if isinstance(values[0], int) else values[0]


def on_chip(chip, core):
    x, y, z = chip // 16, (chip // 4) % 4, chip % 4
    return {"row": y * 2 + x % 2, "col": (x // 2) * 8 + z * 2 + core}


def chunks_of(row, col):
    return jnp.where((row + col) % PANELS < PANELS // 2, MAXNZ, LIGHTNZ)


def kernel(
    band, flags, qtiles, packed, others, raw, tiles, relay, factors, parts, flags1, flags2, following, slots,
    load_sem, own_send, pair_send, relay_send, q_send, q_fwd, flag_send, got1, got2, relay_got, q_got1, q_got2, flag_got, out_sem,
):
    row, col = lax.axis_index("row"), lax.axis_index("col")
    core = col % 2
    odd_row = row % 2
    back1, back2 = (col + PANELS - 1) % PANELS, (col + PANELS - 2) % PANELS
    ahead1, ahead2 = (col + 1) % PANELS, (col + 2) % PANELS
    pair = {"row": row, "col": col + 1 - 2 * core}
    behind = {"row": row, "col": back2}
    row_behind, row_ahead = (row + GRID_ROWS - 2) % GRID_ROWS, (row + 2) % GRID_ROWS
    row_pair = {"row": row + 1 - 2 * odd_row, "col": col}
    n0, n1, n2 = chunks_of(row, col), chunks_of(row, ahead1), chunks_of(row, ahead2)

    load_raw = pltpu.make_async_copy(band, raw, load_sem.at[0])
    load_raw.start()
    load_q = pltpu.make_async_copy(qtiles.at[0], factors.at[0], load_sem.at[1])
    load_q.start()

    me = row * PANELS + col
    outs = []
    first = n0
    for table in OUT:
        code = pick(table, me)
        first = first - code % 16
        outs.append((code // 256, (code // 16) % 16, first, code % 16))
    relayed = n0 - first
    ins = []
    slot = 0
    for table in IN:
        code = pick(table, me)
        ins.append((code // 512, (code // 16) % 32, slot, code % 16))
        slot = slot + code % 16

    barrier = pltpu.get_barrier_semaphore()

    def greet(device):
        pl.semaphore_signal(barrier, inc=1, device_id=device, device_id_type=MESH)

    for device in ({"row": row, "col": ahead1}, {"row": row, "col": ahead2}, pair, {"row": row_ahead, "col": col}, row_pair):
        greet(device)
    expected = 5
    for chip, _, _, count in outs:
        expected = expected + jnp.where(count > 0, 1, 0)
    for chip, _, _, count in ins:
        expected = expected + jnp.where(count > 0, 1, 0)
        target = on_chip(chip, core)

        @pl.when(count > 0)
        def _():
            greet({"row": target["row"], "col": (target["col"] + 2) % PANELS})

    relayed_in, relayed_in1 = jnp.int32(0), jnp.int32(0)
    for table in OUT:
        relayed_in1 = relayed_in1 + pick(table, row * PANELS + ahead1) % 16
        code = pick(table, row * PANELS + ahead2)
        relayed_in = relayed_in + code % 16

        @pl.when(code > 0)
        def _():
            greet(on_chip(code // 256, core))

    following[LR] = LR - 1

    @pl.loop(0, LR)
    def _(t):
        r = LR - 1 - t
        following[r] = jnp.where(flags[r] > 0, r, following[r + 1])

    @pl.loop(0, MAXNZ)
    def _(t):
        before = jnp.where(t == 0, -1, slots[jnp.maximum(t - 1, 0)])
        slots[t] = following[before + 1]

    def remote(src, dst, send, recv, device):
        return pltpu.make_async_remote_copy(
            src_ref=src, dst_ref=dst, send_sem=send, recv_sem=recv, device_id=device, device_id_type=MESH
        )

    def landed(dst, sem):
        pltpu.make_async_copy(dst, dst, sem).wait()

    pl.semaphore_wait(barrier, expected)

    wrapped = jnp.where(row < 2, 1, 0)

    def q_rows(u):
        return pl.ds(u * BS if isinstance(u, int) else pl.multiple_of(u * BS, BS), BS)

    def q_copy(u):
        return remote(
            qtiles.at[wrapped, q_rows(u)], factors.at[2, q_rows(u)], q_send.at[u], q_got2.at[u], {"row": row_behind, "col": col}
        )

    def q_pair_own(u):
        return remote(qtiles.at[0, q_rows(u)], factors.at[1, q_rows(u)], q_fwd.at[u], q_got1.at[u], row_pair)

    def q_pair_forward(u):
        return remote(factors.at[2, q_rows(u)], factors.at[1, q_rows(u)], q_fwd.at[u], q_got1.at[u], row_pair)

    flag_copies = [
        remote(flags, flags1, flag_send.at[0], flag_got.at[0], {"row": row, "col": back1}),
        remote(flags, flags2, flag_send.at[1], flag_got.at[1], behind),
    ]
    for copy in flag_copies:
        copy.start()

    load_raw.wait()

    @pl.loop(0, MAXNZ)
    def _(t):
        @pl.when(t < n0)
        def _():
            tiles[0, t] = raw[slots[t]]

    def own_copy(t):
        return remote(tiles.at[0, t], tiles.at[2, t], own_send.at[t], got2.at[t], behind)

    def own_to_relay(t, chip, at):
        return remote(tiles.at[0, t], relay.at[at], own_send.at[t], relay_got.at[at], on_chip(chip, core))

    def own_to_pair(t):
        return remote(tiles.at[0, t], tiles.at[1, t], pair_send.at[t], got1.at[t], pair)

    def forward_to_pair(t):
        return remote(tiles.at[2, t], tiles.at[1, t], pair_send.at[t], got1.at[t], pair)

    def pass_on(at, chip, t):
        return remote(relay.at[at], tiles.at[2, t], relay_send.at[at], got2.at[t], on_chip(chip, core))

    @pl.when(core == 1)
    def _():
        @pl.loop(0, n0)
        def _(t):
            own_to_pair(t).start()

    load_q.wait()

    def put_away(s, v):
        group = pl.ds(v * GROUP, GROUP)
        return pltpu.make_async_copy(parts.at[s, group], packed.at[s, group], out_sem.at[s, v])

    def multiply(s, v):
        lhs = tiles[s, pl.ds(v * GROUP, GROUP)].reshape(GROUP * BS, WIDTH)
        out = jnp.dot(lhs, factors[s], preferred_element_type=jnp.float32)
        parts[s, pl.ds(v * GROUP, GROUP)] = out.astype(jnp.bfloat16).reshape(GROUP, BS, WIDTH)
        put_away(s, v).start()

    def due(count, tick, ticks):
        return jnp.clip((count * (tick + 1) + ticks - 1) // ticks, 0, count)

    def multiply1(v):
        @pl.loop(v * GROUP, (v + 1) * GROUP)
        def _(u):
            landed(tiles.at[1, u], got1.at[u])

        multiply(1, v)

    def take2(u):
        landed(tiles.at[2, u], got2.at[u])

        @pl.when(core == 0)
        def _():
            forward_to_pair(u).start()

    straight_in = n2 - relayed_in

    def ready2(tick):
        there = due(straight_in, tick - STRAIGHT_LAG, STRAIGHT_TICKS) // GROUP
        return jnp.where(tick < TICK2, 0, there)

    def ready1(tick):
        there = due(n1 - relayed_in1, tick - STRAIGHT_LAG - 1, STRAIGHT_TICKS) // GROUP
        there = jnp.where(core == 0, jnp.minimum(n1 // GROUP, tick - TICK1 + 1), there)
        return jnp.where(tick < TICK1, 0, there)

    @pl.loop(0, TICKS)
    def _(tick):
        @pl.loop(due(QPARTS, tick - 1, Q_TICKS), due(QPARTS, tick, Q_TICKS))
        def _(u):
            q_copy(u).start()

            @pl.when(odd_row == 1)
            def _():
                q_pair_own(u).start()

        for chip, at, t, count in outs:
            @pl.loop(due(count, tick - 1, RELAY_TICKS), due(count, tick, RELAY_TICKS))
            def _(u):
                own_to_relay(t + u, chip, at + u).start()

        @pl.loop(due(n0 - relayed, tick - 1, STRAIGHT_TICKS), due(n0 - relayed, tick, STRAIGHT_TICKS))
        def _(u):
            own_copy(u).start()

        @pl.when((tick % 2 == 1) & (tick < 2 * GROUPS) & (tick // 2 * GROUP < n0))
        def _():
            multiply(0, tick // 2)

        then = tick - LAG

        @pl.when(odd_row == 0)
        def _():
            @pl.loop(due(QPARTS, then - 1, Q_TICKS), due(QPARTS, then, Q_TICKS))
            def _(u):
                landed(factors.at[2, q_rows(u)], q_got2.at[u])
                q_pair_forward(u).start()

        for chip, t, at, count in ins:
            @pl.loop(due(count, then - 1, RELAY_TICKS), due(count, then, RELAY_TICKS))
            def _(u):
                landed(relay.at[at + u], relay_got.at[at + u])
                pass_on(at + u, chip, t + u).start()

        then2 = tick - STRAIGHT_LAG

        @pl.loop(due(straight_in, then2 - 1, STRAIGHT_TICKS), due(straight_in, then2, STRAIGHT_TICKS))
        def _(u):
            take2(u)

        @pl.when((odd_row == 1) & (tick == TICK2))
        def _():
            @pl.loop(0, QPARTS)
            def _(u):
                landed(factors.at[2, q_rows(u)], q_got2.at[u])

        @pl.when(tick == TICK1)
        def _():
            @pl.loop(0, QPARTS)
            def _(u):
                landed(factors.at[1, q_rows(u)], q_got1.at[u])

        @pl.loop(ready2(tick - 1), ready2(tick))
        def _(v):
            multiply(2, v)

        @pl.loop(ready1(tick - 1), ready1(tick))
        def _(v):
            multiply1(v)

    @pl.loop(straight_in, n2)
    def _(u):
        take2(u)

    @pl.loop(ready2(TICKS - 1), n2 // GROUP)
    def _(v):
        multiply(2, v)

    @pl.loop(ready1(TICKS - 1), n1 // GROUP)
    def _(v):
        multiply1(v)

    for copy in flag_copies:
        copy.wait()

    @pl.loop(0, LR)
    def _(r):
        others[0, r] = flags1[r]
        others[1, r] = flags2[r]

    @pl.loop(0, QPARTS)
    def _(u):
        q_copy(u).wait_send()

        @pl.when(odd_row == 1)
        def _():
            q_pair_own(u).wait_send()

        @pl.when(odd_row == 0)
        def _():
            q_pair_forward(u).wait_send()

    @pl.loop(0, n0)
    def _(t):
        own_copy(t).wait_send()

    @pl.loop(0, jnp.where(core == 0, n2, n0))
    def _(t):
        own_to_pair(t).wait_send()

    @pl.loop(0, slot)
    def _(at):
        pass_on(at, 0, 0).wait_send()

    for s, n in enumerate((n0, n1, n2)):
        @pl.loop(0, n // GROUP)
        def _(v):
            put_away(s, v).wait()


def combine(flags, others, packed, product, parts, rows, got, out_sem):
    row, col = lax.axis_index("row"), lax.axis_index("col")
    groups = [chunks_of(row, (col + s) % PANELS) // GROUP for s in range(3)]

    def fetch(s, v):
        group = pl.ds(v * GROUP, GROUP)
        return pltpu.make_async_copy(packed.at[s, group], parts.at[s, group], got.at[s, v])

    def put(r):
        return pltpu.make_async_copy(rows.at[r], product.at[r], out_sem.at[r])

    @pl.loop(0, GROUPS)
    def _(v):
        for s in range(3):
            @pl.when(v < groups[s])
            def _():
                fetch(s, v).start()

    def batch(b, counts):
        for s in range(3):
            @pl.when(b < groups[s])
            def _():
                fetch(s, b).wait()

        for t in range(GROUP):
            r = b * GROUP + t
            there = [flags[r] > 0, others[0, r] > 0, others[1, r] > 0]
            counts = tuple(count + jnp.where(held, 1, 0) for count, held in zip(counts, there))
            at = [jnp.clip(count - 1, 0, MAXNZ - 1) for count in counts]

            @pl.loop(0, BS, step=16)
            def _(h):
                lines = pl.ds(pl.multiple_of(h, 16), 16)
                total = jnp.zeros((16, WIDTH), jnp.float32)
                for s in range(3):
                    total += jnp.where(there[s], parts[s, at[s], lines].astype(jnp.float32), 0.0)
                rows[r, lines] = total.astype(jnp.bfloat16)

            put(r).start()
        return counts

    lax.fori_loop(0, LR // GROUP, batch, (jnp.int32(0),) * 3)

    @pl.loop(0, LR)
    def _(r):
        put(r).wait()


def per_device(apanel, rowmask, qpanel):
    dma = pltpu.SemaphoreType.DMA
    whole = pl.BlockSpec(memory_space=pl.ANY)
    row_flags = rowmask.reshape(LR)
    scalars = pl.BlockSpec(memory_space=pltpu.SMEM)
    packed, others = pl.pallas_call(
        kernel,
        out_shape=(
            jax.ShapeDtypeStruct((3, MAXNZ, BS, WIDTH), jnp.bfloat16),
            jax.ShapeDtypeStruct((2, LR), jnp.int32),
        ),
        in_specs=[whole, scalars, whole],
        out_specs=(whole, scalars),
        scratch_shapes=[
            pltpu.VMEM((LR, BS, WIDTH), jnp.bfloat16),
            pltpu.VMEM((3, MAXNZ, BS, WIDTH), jnp.bfloat16),
            pltpu.VMEM((SLOTS, BS, WIDTH), jnp.bfloat16),
            pltpu.VMEM((3, WIDTH, WIDTH), jnp.bfloat16),
            pltpu.VMEM((3, MAXNZ, BS, WIDTH), jnp.bfloat16),
            pltpu.SMEM((LR,), jnp.int32),
            pltpu.SMEM((LR,), jnp.int32),
            pltpu.SMEM((LR + 1,), jnp.int32),
            pltpu.SMEM((LR,), jnp.int32),
            dma((2,)),
            dma((MAXNZ,)),
            dma((MAXNZ,)),
            dma((SLOTS,)),
            dma((QPARTS,)),
            dma((QPARTS,)),
            dma((2,)),
            dma((MAXNZ,)),
            dma((MAXNZ,)),
            dma((SLOTS,)),
            dma((QPARTS,)),
            dma((QPARTS,)),
            dma((2,)),
            dma((3, GROUPS)),
        ],
        compiler_params=pltpu.CompilerParams(collective_id=0, has_side_effects=True, vmem_limit_bytes=60 << 20),
    )(apanel.reshape(LR, BS, WIDTH), row_flags, qpanel)
    product = pl.pallas_call(
        combine,
        out_shape=jax.ShapeDtypeStruct((LR, BS, WIDTH), jnp.bfloat16),
        in_specs=[scalars, scalars, whole],
        out_specs=whole,
        scratch_shapes=[
            pltpu.VMEM((3, MAXNZ, BS, WIDTH), jnp.bfloat16),
            pltpu.VMEM((LR, BS, WIDTH), jnp.bfloat16),
            dma((3, GROUPS)),
            dma((LR,)),
        ],
        compiler_params=pltpu.CompilerParams(vmem_limit_bytes=60 << 20),
    )(row_flags, others, packed)
    return product.reshape(LR * BS, WIDTH)


def solution(mesh):
    in_specs = (P("row", "col"), P("row", "col"), P(None, "row", "col"))
    return jax.shard_map(per_device, mesh=mesh, in_specs=in_specs, out_specs=P("row", "col"), check_vma=False)
```

```python
import jax
import jax.numpy as jnp
from jax import lax
from jax.experimental import pallas as pl
from jax.experimental.pallas import tpu as pltpu
from jax.sharding import PartitionSpec as P

BS = 128
LR = 32
WIDTH = 1024
MAXNZ = 24
LIGHTNZ = 8
PANELS = 16
GRID_ROWS = 8
GROUP = 4
GROUPS = MAXNZ // GROUP
QPARTS = WIDTH // BS
MESH = pl.DeviceIdType.MESH

OUT = [
    [
        518, 518, 12806, 12806, 5, 5, 1540, 1540, 4865, 4865, 0, 0, 0, 0, 0, 0,
        4614, 4614, 7174, 7174, 4102, 4102, 5634, 0, 13137, 13137, 0, 0, 0, 0, 12322, 0,
        1798, 1798, 13318, 13318, 1030, 1030, 0, 0, 9729, 9729, 0, 0, 0, 0, 9222, 9222,
        5894, 5894, 9318, 9318, 5122, 0, 0, 0, 13825, 13825, 0, 0, 9474, 0, 13414, 13414,
        2822, 2822, 2596, 2596, 0, 0, 0, 0, 11009, 11009, 0, 0, 9509, 9477, 6741, 6741,
        6918, 6918, 0, 6818, 0, 0, 0, 0, 15105, 15105, 0, 13842, 2405, 2405, 2662, 2662,
        3638, 3638, 0, 0, 0, 0, 0, 0, 8017, 8017, 8198, 8198, 7430, 7430, 11270, 11270,
        12044, 0, 0, 0, 0, 0, 0, 0, 0, 16140, 12374, 12342, 12550, 12550, 15366, 15366,
    ],
    [
        774, 774, 3075, 3075, 3332, 3332, 3587, 3587, 0, 0, 0, 0, 0, 0, 0, 0,
        8966, 8966, 8707, 8707, 8451, 8451, 0, 0, 0, 0, 0, 0, 0, 0, 0, 0,
        14086, 14086, 2562, 2562, 6402, 6402, 0, 0, 0, 0, 0, 0, 0, 0, 8755, 8755,
        9990, 9990, 6659, 6659, 0, 0, 0, 0, 0, 0, 0, 0, 0, 0, 1698, 1698,
        14854, 14854, 3123, 3123, 0, 0, 0, 0, 0, 0, 0, 0, 6434, 6434, 10276, 10276,
        10758, 10758, 0, 0, 0, 0, 0, 0, 0, 0, 0, 0, 14339, 14339, 14387, 14387,
        3846, 3846, 0, 0, 0, 0, 0, 0, 0, 0, 10338, 10338, 8499, 8499, 8803, 8803,
        7686, 0, 0, 0, 0, 0, 0, 0, 0, 15878, 15875, 15971, 3394, 3394, 3731, 3731,
    ],
    [
        13061, 13061, 0, 0, 0, 0, 12290, 12290, 0, 0, 0, 0, 0, 0, 0, 0,
        4885, 4885, 0, 0, 0, 0, 0, 0, 0, 0, 0, 0, 0, 0, 0, 0,
        1605, 1605, 1681, 1681, 2305, 2305, 0, 0, 0, 0, 0, 0, 0, 0, 0, 0,
        5669, 5637, 0, 0, 0, 0, 0, 0, 0, 0, 0, 0, 0, 0, 12353, 12321,
        2325, 2325, 6706, 6706, 0, 0, 0, 0, 0, 0, 0, 0, 10242, 10242, 0, 0,
        7941, 7941, 0, 0, 0, 0, 0, 0, 0, 0, 0, 0, 6465, 6465, 0, 0,
        15125, 15125, 0, 0, 0, 0, 0, 0, 0, 0, 11777, 11777, 0, 0, 0, 0,
        0, 0, 0, 0, 0, 0, 0, 0, 0, 0, 0, 0, 3169, 3169, 0, 0,
    ],
]
IN = [
    [
        821, 821, 0, 0, 18214, 18214, 18118, 18118, 22822, 22822, 8947, 8947, 8435, 8435, 26310, 26310,
        8998, 8998, 0, 0, 26406, 26406, 1649, 1649, 1266, 1266, 31526, 31526, 294, 294, 18037, 18037,
        2854, 2854, 0, 0, 1348, 1348, 20262, 20262, 19750, 19750, 27234, 21301, 3697, 3697, 28358, 28358,
        11106, 0, 0, 0, 9570, 28277, 28454, 28454, 2342, 2342, 0, 0, 11889, 11889, 20166, 20166,
        0, 0, 2801, 2801, 2306, 2306, 22310, 22310, 21234, 21234, 0, 0, 30406, 30406, 5745, 5745,
        0, 0, 2818, 2818, 10483, 10483, 30502, 30502, 29443, 29443, 0, 0, 22214, 22214, 13937, 13937,
        243, 243, 756, 756, 1299, 1299, 24262, 24262, 23846, 23846, 0, 0, 22769, 22769, 32460, 0,
        8486, 8486, 23334, 23334, 32358, 0, 30325, 30325, 32038, 32038, 0, 0, 30963, 15974, 0, 16076,
    ],
    [
        0, 0, 0, 0, 0, 0, 0, 0, 0, 0, 23283, 23283, 19699, 19699, 0, 0,
        0, 0, 0, 0, 0, 0, 26229, 26229, 25698, 27889, 0, 0, 0, 0, 9841, 9841,
        0, 0, 0, 0, 20085, 20085, 0, 0, 10534, 10534, 21301, 0, 0, 0, 0, 0,
        0, 0, 0, 0, 28277, 0, 0, 0, 27942, 27942, 0, 0, 0, 29026, 0, 0,
        0, 0, 22133, 22133, 4420, 4420, 0, 0, 21748, 21748, 0, 0, 0, 0, 0, 0,
        0, 0, 21266, 21266, 4338, 4338, 0, 0, 29939, 29939, 0, 0, 0, 0, 24181, 24181,
        4371, 4371, 31490, 31490, 24358, 24358, 0, 0, 0, 0, 0, 0, 0, 0, 0, 0,
        0, 0, 0, 0, 0, 0, 7793, 7793, 0, 0, 0, 0, 0, 30963, 0, 0,
    ],
    [
        0, 0, 0, 0, 0, 0, 0, 0, 0, 0, 0, 0, 23795, 23795, 0, 0,
        0, 0, 0, 0, 0, 0, 0, 0, 27889, 31014, 0, 0, 0, 0, 0, 0,
        0, 0, 0, 0, 2289, 2289, 0, 0, 0, 0, 0, 0, 0, 0, 0, 0,
        0, 0, 0, 0, 0, 0, 0, 0, 0, 0, 0, 0, 0, 0, 0, 0,
        0, 0, 29493, 29493, 29990, 29990, 0, 0, 22786, 22786, 0, 0, 0, 0, 0, 0,
        0, 0, 29425, 29425, 21813, 21813, 0, 0, 0, 0, 0, 0, 0, 0, 0, 0,
        31473, 31473, 0, 0, 31987, 31987, 0, 0, 0, 0, 0, 0, 0, 0, 0, 0,
        0, 0, 0, 0, 0, 0, 0, 0, 0, 0, 0, 0, 0, 0, 0, 0,
    ],
    [
        0, 0, 0, 0, 0, 0, 0, 0, 0, 0, 0, 0, 0, 0, 0, 0,
        0, 0, 0, 0, 0, 0, 0, 0, 31014, 0, 0, 0, 0, 0, 0, 0,
        0, 0, 0, 0, 27906, 27906, 0, 0, 0, 0, 0, 0, 0, 0, 0, 0,
        0, 0, 0, 0, 0, 0, 0, 0, 0, 0, 0, 0, 0, 0, 0, 0,
        0, 0, 0, 0, 0, 0, 0, 0, 0, 0, 0, 0, 0, 0, 0, 0,
        0, 0, 0, 0, 0, 12386, 0, 0, 0, 0, 0, 0, 0, 0, 0, 0,
        0, 0, 0, 0, 0, 0, 0, 0, 0, 0, 0, 0, 0, 0, 0, 0,
        0, 0, 0, 0, 0, 0, 0, 0, 0, 0, 0, 0, 0, 0, 0, 0,
    ],
]
SLOTS = 12

TICKS = 12
Q_TICKS = 8
RELAY_TICKS = 8
STRAIGHT_TICKS = 10
LAG = 1
STRAIGHT_LAG = 2
TICK2 = Q_TICKS + LAG
TICK1 = TICK2 + LAG + 1


def pick(values, at):
    bit = 1
    while len(values) > 1:
        odd = (at // bit) % 2 == 1
        values = [
            a if isinstance(a, int) and isinstance(b, int) and a == b else jnp.where(odd, b, a)
            for a, b in zip(values[::2], values[1::2])
        ]
        bit *= 2
    return jnp.int32(values[0]) if isinstance(values[0], int) else values[0]


def on_chip(chip, core):
    x, y, z = chip // 16, (chip // 4) % 4, chip % 4
    return {"row": y * 2 + x % 2, "col": (x // 2) * 8 + z * 2 + core}


def chunks_of(row, col):
    return jnp.where((row + col) % PANELS < PANELS // 2, MAXNZ, LIGHTNZ)


def kernel(
    band, flags, qtiles, packed, others, raw, tiles, relay, factors, parts, flags1, flags2, following, slots,
    load_sem, own_send, pair_send, relay_send, q_send, q_fwd, flag_send, got1, got2, relay_got, q_got1, q_got2, flag_got, out_sem,
):
    row, col = lax.axis_index("row"), lax.axis_index("col")
    core = col % 2
    odd_row = row % 2
    back1, back2 = (col + PANELS - 1) % PANELS, (col + PANELS - 2) % PANELS
    ahead1, ahead2 = (col + 1) % PANELS, (col + 2) % PANELS
    pair = {"row": row, "col": col + 1 - 2 * core}
    behind = {"row": row, "col": back2}
    row_behind, row_ahead = (row + GRID_ROWS - 2) % GRID_ROWS, (row + 2) % GRID_ROWS
    row_pair = {"row": row + 1 - 2 * odd_row, "col": col}
    n0, n1, n2 = chunks_of(row, col), chunks_of(row, ahead1), chunks_of(row, ahead2)

    load_raw = pltpu.make_async_copy(band, raw, load_sem.at[0])
    load_raw.start()
    load_q = pltpu.make_async_copy(qtiles.at[0], factors.at[0], load_sem.at[1])
    load_q.start()

    me = row * PANELS + col
    outs = []
    first = n0
    for table in OUT:
        code = pick(table, me)
        first = first - code % 16
        outs.append((code // 256, (code // 16) % 16, first, code % 16))
    relayed = n0 - first
    ins = []
    slot = 0
    for table in IN:
        code = pick(table, me)
        ins.append((code // 512, (code // 16) % 32, slot, code % 16))
        slot = slot + code % 16

    barrier = pltpu.get_barrier_semaphore()

    def greet(device):
        pl.semaphore_signal(barrier, inc=1, device_id=device, device_id_type=MESH)

    for device in ({"row": row, "col": ahead1}, {"row": row, "col": ahead2}, pair, {"row": row_ahead, "col": col}, row_pair):
        greet(device)
    expected = 5
    for chip, _, _, count in outs:
        expected = expected + jnp.where(count > 0, 1, 0)
    for chip, _, _, count in ins:
        expected = expected + jnp.where(count > 0, 1, 0)
        target = on_chip(chip, core)

        @pl.when(count > 0)
        def _():
            greet({"row": target["row"], "col": (target["col"] + 2) % PANELS})

    relayed_in, relayed_in1 = jnp.int32(0), jnp.int32(0)
    for table in OUT:
        relayed_in1 = relayed_in1 + pick(table, row * PANELS + ahead1) % 16
        code = pick(table, row * PANELS + ahead2)
        relayed_in = relayed_in + code % 16

        @pl.when(code > 0)
        def _():
            greet(on_chip(code // 256, core))

    following[LR] = LR - 1

    @pl.loop(0, LR)
    def _(t):
        r = LR - 1 - t
        following[r] = jnp.where(flags[r] > 0, r, following[r + 1])

    @pl.loop(0, MAXNZ)
    def _(t):
        before = jnp.where(t == 0, -1, slots[jnp.maximum(t - 1, 0)])
        slots[t] = following[before + 1]

    def remote(src, dst, send, recv, device):
        return pltpu.make_async_remote_copy(
            src_ref=src, dst_ref=dst, send_sem=send, recv_sem=recv, device_id=device, device_id_type=MESH
        )

    def landed(dst, sem):
        pltpu.make_async_copy(dst, dst, sem).wait()

    pl.semaphore_wait(barrier, expected)

    wrapped = jnp.where(row < 2, 1, 0)

    def q_rows(u):
        return pl.ds(u * BS if isinstance(u, int) else pl.multiple_of(u * BS, BS), BS)

    def q_copy(u):
        return remote(
            qtiles.at[wrapped, q_rows(u)], factors.at[2, q_rows(u)], q_send.at[u], q_got2.at[u], {"row": row_behind, "col": col}
        )

    def q_pair_own(u):
        return remote(qtiles.at[0, q_rows(u)], factors.at[1, q_rows(u)], q_fwd.at[u], q_got1.at[u], row_pair)

    def q_pair_forward(u):
        return remote(factors.at[2, q_rows(u)], factors.at[1, q_rows(u)], q_fwd.at[u], q_got1.at[u], row_pair)

    flag_copies = [
        remote(flags, flags1, flag_send.at[0], flag_got.at[0], {"row": row, "col": back1}),
        remote(flags, flags2, flag_send.at[1], flag_got.at[1], behind),
    ]
    for copy in flag_copies:
        copy.start()

    load_raw.wait()

    @pl.loop(0, MAXNZ)
    def _(t):
        @pl.when(t < n0)
        def _():
            tiles[0, t] = raw[slots[t]]

    def own_copy(t):
        return remote(tiles.at[0, t], tiles.at[2, t], own_send.at[t], got2.at[t], behind)

    def own_to_relay(t, chip, at):
        return remote(tiles.at[0, t], relay.at[at], own_send.at[t], relay_got.at[at], on_chip(chip, core))

    def own_to_pair(t):
        return remote(tiles.at[0, t], tiles.at[1, t], pair_send.at[t], got1.at[t], pair)

    def forward_to_pair(t):
        return remote(tiles.at[2, t], tiles.at[1, t], pair_send.at[t], got1.at[t], pair)

    def pass_on(at, chip, t):
        return remote(relay.at[at], tiles.at[2, t], relay_send.at[at], got2.at[t], on_chip(chip, core))

    @pl.when(core == 1)
    def _():
        @pl.loop(0, n0)
        def _(t):
            own_to_pair(t).start()

    load_q.wait()

    def put_away(s, v):
        group = pl.ds(v * GROUP, GROUP)
        return pltpu.make_async_copy(parts.at[s, group], packed.at[s, group], out_sem.at[s, v])

    def multiply(s, v):
        lhs = tiles[s, pl.ds(v * GROUP, GROUP)].reshape(GROUP * BS, WIDTH)
        out = jnp.dot(lhs, factors[s], preferred_element_type=jnp.float32)
        parts[s, pl.ds(v * GROUP, GROUP)] = out.astype(jnp.bfloat16).reshape(GROUP, BS, WIDTH)
        put_away(s, v).start()

    def due(count, tick, ticks):
        return jnp.clip((count * (tick + 1) + ticks - 1) // ticks, 0, count)

    def multiply1(v):
        @pl.loop(v * GROUP, (v + 1) * GROUP)
        def _(u):
            landed(tiles.at[1, u], got1.at[u])

        multiply(1, v)

    def take2(u):
        landed(tiles.at[2, u], got2.at[u])

        @pl.when(core == 0)
        def _():
            forward_to_pair(u).start()

    straight_in = n2 - relayed_in

    def ready2(tick):
        there = due(straight_in, tick - STRAIGHT_LAG, STRAIGHT_TICKS) // GROUP
        return jnp.where(tick < TICK2, 0, there)

    def ready1(tick):
        there = due(n1 - relayed_in1, tick - STRAIGHT_LAG - 1, STRAIGHT_TICKS) // GROUP
        there = jnp.where(core == 0, jnp.minimum(n1 // GROUP, tick - TICK1 + 1), there)
        return jnp.where(tick < TICK1, 0, there)

    @pl.loop(0, TICKS)
    def _(tick):
        @pl.loop(due(QPARTS, tick - 1, Q_TICKS), due(QPARTS, tick, Q_TICKS))
        def _(u):
            q_copy(u).start()

            @pl.when(odd_row == 1)
            def _():
                q_pair_own(u).start()

        for chip, at, t, count in outs:
            @pl.loop(due(count, tick - 1, RELAY_TICKS), due(count, tick, RELAY_TICKS))
            def _(u):
                own_to_relay(t + u, chip, at + u).start()

        @pl.loop(due(n0 - relayed, tick - 1, STRAIGHT_TICKS), due(n0 - relayed, tick, STRAIGHT_TICKS))
        def _(u):
            own_copy(u).start()

        @pl.when((tick % 2 == 1) & (tick < 2 * GROUPS) & (tick // 2 * GROUP < n0))
        def _():
            multiply(0, tick // 2)

        then = tick - LAG

        @pl.when(odd_row == 0)
        def _():
            @pl.loop(due(QPARTS, then - 1, Q_TICKS), due(QPARTS, then, Q_TICKS))
            def _(u):
                landed(factors.at[2, q_rows(u)], q_got2.at[u])
                q_pair_forward(u).start()

        for chip, t, at, count in ins:
            @pl.loop(due(count, then - 1, RELAY_TICKS), due(count, then, RELAY_TICKS))
            def _(u):
                landed(relay.at[at + u], relay_got.at[at + u])
                pass_on(at + u, chip, t + u).start()

        then2 = tick - STRAIGHT_LAG

        @pl.loop(due(straight_in, then2 - 1, STRAIGHT_TICKS), due(straight_in, then2, STRAIGHT_TICKS))
        def _(u):
            take2(u)

        @pl.when((odd_row == 1) & (tick == TICK2))
        def _():
            @pl.loop(0, QPARTS)
            def _(u):
                landed(factors.at[2, q_rows(u)], q_got2.at[u])

        @pl.when(tick == TICK1)
        def _():
            @pl.loop(0, QPARTS)
            def _(u):
                landed(factors.at[1, q_rows(u)], q_got1.at[u])

        @pl.loop(ready2(tick - 1), ready2(tick))
        def _(v):
            multiply(2, v)

        @pl.loop(ready1(tick - 1), ready1(tick))
        def _(v):
            multiply1(v)

    @pl.loop(straight_in, n2)
    def _(u):
        take2(u)

    @pl.loop(ready2(TICKS - 1), n2 // GROUP)
    def _(v):
        multiply(2, v)

    @pl.loop(ready1(TICKS - 1), n1 // GROUP)
    def _(v):
        multiply1(v)

    for copy in flag_copies:
        copy.wait()

    @pl.loop(0, LR)
    def _(r):
        others[0, r] = flags1[r]
        others[1, r] = flags2[r]

    @pl.loop(0, QPARTS)
    def _(u):
        q_copy(u).wait_send()

        @pl.when(odd_row == 1)
        def _():
            q_pair_own(u).wait_send()

        @pl.when(odd_row == 0)
        def _():
            q_pair_forward(u).wait_send()

    @pl.loop(0, n0)
    def _(t):
        own_copy(t).wait_send()

    @pl.loop(0, jnp.where(core == 0, n2, n0))
    def _(t):
        own_to_pair(t).wait_send()

    @pl.loop(0, slot)
    def _(at):
        pass_on(at, 0, 0).wait_send()

    for s, n in enumerate((n0, n1, n2)):
        @pl.loop(0, n // GROUP)
        def _(v):
            put_away(s, v).wait()


def combine(flags, others, packed, product, parts, rows, got, out_sem):
    row, col = lax.axis_index("row"), lax.axis_index("col")
    groups = [chunks_of(row, (col + s) % PANELS) // GROUP for s in range(3)]

    def fetch(s, v):
        group = pl.ds(v * GROUP, GROUP)
        return pltpu.make_async_copy(packed.at[s, group], parts.at[s, group], got.at[s, v])

    def put(r):
        return pltpu.make_async_copy(rows.at[r], product.at[r], out_sem.at[r])

    @pl.loop(0, GROUPS)
    def _(v):
        for s in range(3):
            @pl.when(v < groups[s])
            def _():
                fetch(s, v).start()

    @pl.loop(0, BS, step=16)
    def _(h):
        for s in range(3):
            parts[s, MAXNZ, pl.ds(pl.multiple_of(h, 16), 16)] = jnp.zeros((16, WIDTH), jnp.bfloat16)

    def batch(b, counts):
        for s in range(3):
            @pl.when(b < groups[s])
            def _():
                fetch(s, b).wait()

        for t in range(GROUP):
            r = b * GROUP + t
            there = [flags[r] > 0, others[0, r] > 0, others[1, r] > 0]
            counts = tuple(count + jnp.where(held, 1, 0) for count, held in zip(counts, there))
            at = [jnp.where(held, jnp.clip(count - 1, 0, MAXNZ - 1), MAXNZ) for count, held in zip(counts, there)]

            @pl.loop(0, BS, step=16, unroll=4)
            def _(h):
                lines = pl.ds(pl.multiple_of(h, 16), 16)
                terms = [parts[s, at[s], lines].astype(jnp.float32) for s in range(3)]
                rows[r, lines] = (terms[0] + terms[1] + terms[2]).astype(jnp.bfloat16)

            put(r).start()
        return counts

    lax.fori_loop(0, LR // GROUP, batch, (jnp.int32(0),) * 3)

    @pl.loop(0, LR)
    def _(r):
        put(r).wait()


def per_device(apanel, rowmask, qpanel):
    dma = pltpu.SemaphoreType.DMA
    whole = pl.BlockSpec(memory_space=pl.ANY)
    row_flags = rowmask.reshape(LR)
    scalars = pl.BlockSpec(memory_space=pltpu.SMEM)
    packed, others = pl.pallas_call(
        kernel,
        out_shape=(
            jax.ShapeDtypeStruct((3, MAXNZ, BS, WIDTH), jnp.bfloat16),
            jax.ShapeDtypeStruct((2, LR), jnp.int32),
        ),
        in_specs=[whole, scalars, whole],
        out_specs=(whole, scalars),
        scratch_shapes=[
            pltpu.VMEM((LR, BS, WIDTH), jnp.bfloat16),
            pltpu.VMEM((3, MAXNZ, BS, WIDTH), jnp.bfloat16),
            pltpu.VMEM((SLOTS, BS, WIDTH), jnp.bfloat16),
            pltpu.VMEM((3, WIDTH, WIDTH), jnp.bfloat16),
            pltpu.VMEM((3, MAXNZ, BS, WIDTH), jnp.bfloat16),
            pltpu.SMEM((LR,), jnp.int32),
            pltpu.SMEM((LR,), jnp.int32),
            pltpu.SMEM((LR + 1,), jnp.int32),
            pltpu.SMEM((LR,), jnp.int32),
            dma((2,)),
            dma((MAXNZ,)),
            dma((MAXNZ,)),
            dma((SLOTS,)),
            dma((QPARTS,)),
            dma((QPARTS,)),
            dma((2,)),
            dma((MAXNZ,)),
            dma((MAXNZ,)),
            dma((SLOTS,)),
            dma((QPARTS,)),
            dma((QPARTS,)),
            dma((2,)),
            dma((3, GROUPS)),
        ],
        compiler_params=pltpu.CompilerParams(collective_id=0, has_side_effects=True, vmem_limit_bytes=60 << 20),
    )(apanel.reshape(LR, BS, WIDTH), row_flags, qpanel)
    product = pl.pallas_call(
        combine,
        out_shape=jax.ShapeDtypeStruct((LR, BS, WIDTH), jnp.bfloat16),
        in_specs=[scalars, scalars, whole],
        out_specs=whole,
        scratch_shapes=[
            pltpu.VMEM((3, MAXNZ + 1, BS, WIDTH), jnp.bfloat16),
            pltpu.VMEM((LR, BS, WIDTH), jnp.bfloat16),
            dma((3, GROUPS)),
            dma((LR,)),
        ],
        compiler_params=pltpu.CompilerParams(vmem_limit_bytes=60 << 20),
    )(row_flags, others, packed)
    return product.reshape(LR * BS, WIDTH)


def solution(mesh):
    in_specs = (P("row", "col"), P("row", "col"), P(None, "row", "col"))
    return jax.shard_map(per_device, mesh=mesh, in_specs=in_specs, out_specs=P("row", "col"), check_vma=False)
```
